32 devices in a mesh: context: 16 (over z, x, core), tensor: 2 (over y).
Axes of the slice: x: 2, y: 2, z: 4, core: 2. Of those that a mesh axis runs over, the one named last changes fastest.
Arguments:
- query: bfloat16 [6144, 4096], P('context', 'tensor'), may hold values from -16 to 16
- keys: bfloat16 [6144, 1024], P('context', 'tensor'), may hold values from -16 to 16
- values: bfloat16 [6144, 1024], P('context', 'tensor'), may hold values from -6 to 6
- vert_cols: int32 [8, 16], P('tensor'), may hold values from 0 to 6080, as said below
- slash_off: int32 [8, 15], P('tensor'), may hold values from 1 to 48, as said below
- doc_ids: int32 [96], replicated, may hold values from 0 to 3, never falling along the last dimension, each value on 1 to 48 neighbouring positions
- out_weight: bfloat16 [4096, 4096], P('tensor'), may hold values from -0.09375 to 0.09375
Outputs:
- layer_out: bfloat16 [6144, 4096], P(('context', 'tensor'))
The draws below stay inside these ranges and needn't reach their ends.
Inputs may be any that keep to these rules, and one draw needn't show every extreme that they name: `vert_cols`: within one kv head the columns are distinct multiples of 64; every head has column 0. `slash_off`: within one kv head the offsets are distinct. `doc_ids`: never falling along the blocks; one document spans 1 to 48 blocks.
All inputs are finite; a program needn't handle non-finite values.
Results may differ from the reference program's by a relative error of at most 0.009.
Values may be sent and summed in bfloat16 or wider, within the bound.
A program may use at most 192 MiB of HBM per device.

```python
import math
import jax
import jax.numpy as jnp
import numpy as np
from jax import lax

D = 4096
QH = 32
KVH = 8
HD = 128
BLOCK = 64
NV = 16
NS = 15
HOPS = 8
DOCS = 4
QB = 6
TOKENS = 6144
NKB = 96
DOC_MOST = 48
N_TENSOR = 2


def draw_query(key, part):
    key = jax.random.fold_in(key, 1)
    drawn = jnp.clip(jax.random.normal(key, (TOKENS, QH * HD), jnp.float32), -6.0, 6.0)
    return drawn.astype(jnp.bfloat16)


def draw_keys(key, part):
    key = jax.random.fold_in(key, 2)
    drawn = jnp.clip(jax.random.normal(key, (TOKENS, KVH * HD), jnp.float32), -6.0, 6.0)
    return drawn.astype(jnp.bfloat16)


def draw_vert_cols(key, part):
    key = jax.random.fold_in(key, 3)
    head_keys = jax.random.split(key, KVH)

    def one_head(head_key):
        return jax.random.permutation(head_key, NKB - 2)[:NV - 1] + 1
    picks = jax.vmap(one_head)(head_keys).astype(jnp.int32)
    late_head = jax.random.randint(jax.random.fold_in(key, 9), (), 0, KVH)
    last_col = jnp.where(jnp.arange(KVH) == late_head, NKB - 1, picks[:, -1]).astype(jnp.int32)
    picks = picks.at[:, -1].set(last_col)
    every = jnp.concatenate([jnp.zeros((KVH, 1), jnp.int32), picks], axis=1)
    return (jnp.sort(every, axis=1) * BLOCK).astype(jnp.int32)


def draw_slash_off(key, part):
    key = jax.random.fold_in(key, 4)
    reach = HOPS * QB
    head_keys = jax.random.split(key, KVH)

    def one_head(head_key):
        return jax.random.permutation(head_key, reach - 1)[:NS] + 1
    picks = jax.vmap(one_head)(head_keys).astype(jnp.int32)
    far_head = jax.random.randint(jax.random.fold_in(key, 9), (), 0, KVH)
    first_col = jnp.where(jnp.arange(KVH) == far_head, reach, picks[:, 0]).astype(jnp.int32)
    return picks.at[:, 0].set(first_col).astype(jnp.int32)


def shard_levels(rng, dims, shards, least, top_value):
    factor_of = 1.0
    for dim, blocks in shards:
        heights = jax.random.uniform(jax.random.fold_in(jax.random.fold_in(rng, 6), dim), (blocks,), jnp.float32, least / len(shards), top_value / len(shards))
        factor_of = factor_of * jnp.repeat(jnp.exp(heights), dims[dim] // blocks).reshape((-1,) + (1,) * (len(dims) - 1 - dim))
    return factor_of


def split_up(count, total, limit, skew):
    loads = [(1 << 20) // math.isqrt(standing ** skew) + 1 for standing in range(2, count + 1)]
    surplus, counts = total - limit - (count - 1), [1] * (count - 1)
    while surplus > 0:
        candidates = [i for i in range(count - 1) if counts[i] < limit]
        pool, budget = sum([loads[i] for i in candidates]), surplus
        for i in candidates:
            extra = min(limit - counts[i], max(1, budget * loads[i] // pool), surplus)
            counts[i] = counts[i] + extra
            surplus = surplus - extra
    return np.array([limit] + counts)


def uneven_parts(rng, number_of, total, most, slope):
    if number_of == 2:
        one = jax.random.randint(rng, (), max(1, total - most), min(most, total - 1) + 1)
        return jnp.stack([one, total - one])
    sizes = jnp.asarray(split_up(number_of, total, most, slope), jnp.int32)
    twos = (number_of - 1) // 2
    donor, sink = sizes[1:1 + 2 * twos:2], sizes[2:2 + 2 * twos:2]
    margin = jnp.minimum(donor - 1, most - sink)
    shifted = jax.random.randint(jax.random.fold_in(rng, 1), (twos,), 0, 1 << 20) % (margin + 1)
    sizes = sizes.at[1:1 + 2 * twos:2].set(donor - shifted).at[2:2 + 2 * twos:2].set(sink + shifted)
    return sizes[jax.random.permutation(jax.random.fold_in(rng, 2), number_of)]


def noise(own_key, shape, scale, most, cuts=(), held_as=jnp.bfloat16):
    values = scale * jax.random.normal(own_key, shape, jnp.float32)
    if cuts:
        values = values * shard_levels(own_key, shape, cuts, -0.22, 0.18)
    return jnp.clip(values, -most, most).astype(held_as)


def setup_inputs(seed: int = 0) -> dict:
    seeds = jax.random.split(jax.random.key(seed), 8)
    query = draw_query(jax.random.fold_in(seeds[7], 71), 0)
    keys = draw_keys(jax.random.fold_in(seeds[7], 71), 0)
    values = noise(seeds[2], (TOKENS, KVH * HD), 1.0, 6.0, ((0, 16), (1, 2)))
    vert_cols = draw_vert_cols(jax.random.fold_in(seeds[7], 71), 0)
    slash_off = draw_slash_off(jax.random.fold_in(seeds[7], 71), 0)
    doc_ids = jnp.searchsorted(jnp.cumsum(uneven_parts(seeds[5], DOCS, NKB, DOC_MOST, 1)), jnp.arange(NKB), side="right").astype(jnp.int32)
    out_weight = noise(seeds[6], (QH * HD, D), (QH * HD) ** -0.5, 0.09375, ((0, 2),))
    return dict(query=query, keys=keys, values=values, vert_cols=vert_cols, slash_off=slash_off, doc_ids=doc_ids, out_weight=out_weight)


floor_score = -1.0e30


def reference(query, keys, values, vert_cols, slash_off, doc_ids, out_weight):
    group_size = QH // KVH
    scale = HD ** -0.5
    key_blocks = keys.reshape(NKB, BLOCK, KVH, HD)
    value_blocks = values.reshape(NKB, BLOCK, KVH, HD)
    query_blocks = query.reshape(NKB, BLOCK, KVH, group_size, HD)
    head_ids = jnp.arange(KVH, dtype=jnp.int32)[:, None]
    column_blocks = (vert_cols // BLOCK).astype(jnp.int32)
    column_keys = key_blocks[column_blocks, :, head_ids].astype(jnp.float32)
    column_values = value_blocks[column_blocks, :, head_ids].astype(jnp.float32)
    causal_mask = jnp.arange(BLOCK)[:, None] >= jnp.arange(BLOCK)[None, :]

    def attend(block):
        q_part = query_blocks[block].astype(jnp.float32)
        diag_keys = key_blocks[block].astype(jnp.float32)
        diag_values = value_blocks[block].astype(jnp.float32)
        my_doc = doc_ids[block]
        band_index = (block - slash_off).astype(jnp.int32)
        band_safe = jnp.maximum(band_index, 0).astype(jnp.int32)
        band_live = (band_index >= 0) & (doc_ids[band_safe] == my_doc)
        band_keys = key_blocks[band_safe, :, head_ids].astype(jnp.float32)
        band_values = value_blocks[band_safe, :, head_ids].astype(jnp.float32)
        on_slash = jnp.any((block - column_blocks)[:, :, None] == slash_off[:, None, :], axis=-1)
        same_doc = doc_ids[column_blocks] == my_doc
        column_live = (column_blocks < block) & jnp.logical_not(on_slash & same_doc)
        score_diag = jnp.einsum("rghd,cgd->ghrc", q_part, diag_keys) * scale
        score_diag = jnp.where(causal_mask, score_diag, floor_score)
        score_band = jnp.einsum("rghd,gncd->ghrnc", q_part, band_keys) * scale
        score_band = jnp.where(band_live[:, None, None, :, None], score_band, floor_score)
        score_cols = jnp.einsum("rghd,gncd->ghrnc", q_part, column_keys) * scale
        score_cols = jnp.where(column_live[:, None, None, :, None], score_cols, floor_score)
        top = jnp.maximum(jnp.max(score_diag, axis=-1),
                          jnp.maximum(jnp.max(score_band, axis=(-2, -1)), jnp.max(score_cols, axis=(-2, -1))))
        weight_diag = jnp.where(causal_mask, jnp.exp(score_diag - top[..., None]), 0.0)
        weight_band = jnp.where(band_live[:, None, None, :, None], jnp.exp(score_band - top[..., None, None]), 0.0)
        weight_cols = jnp.where(column_live[:, None, None, :, None], jnp.exp(score_cols - top[..., None, None]), 0.0)
        total = jnp.sum(weight_diag, axis=-1) + jnp.sum(weight_band, axis=(-2, -1)) + jnp.sum(weight_cols, axis=(-2, -1))
        rounded_diag = weight_diag.astype(jnp.bfloat16).astype(jnp.float32)
        rounded_band = weight_band.astype(jnp.bfloat16).astype(jnp.float32)
        rounded_cols = weight_cols.astype(jnp.bfloat16).astype(jnp.float32)
        summed = jnp.einsum("ghrc,cgd->rghd", rounded_diag, diag_values)
        summed = summed + jnp.einsum("ghrnc,gncd->rghd", rounded_band, band_values)
        summed = summed + jnp.einsum("ghrnc,gncd->rghd", rounded_cols, column_values)
        return (summed / jnp.transpose(total, (2, 0, 1))[..., None]).astype(jnp.bfloat16)

    attended = lax.map(attend, jnp.arange(NKB, dtype=jnp.int32)).reshape(TOKENS, QH * HD)
    width = QH * HD // N_TENSOR
    weight_parts = out_weight.reshape(N_TENSOR, width, D).astype(jnp.float32)

    def project(row_block):
        rows_here = lax.dynamic_slice_in_dim(attended, row_block * BLOCK, BLOCK, 0)
        grouped = rows_here.reshape(BLOCK, N_TENSOR, width).astype(jnp.float32)
        partial_terms = jnp.einsum("rtw,twd->rtd", grouped, weight_parts).astype(jnp.bfloat16)
        return jnp.sum(partial_terms.astype(jnp.float32), axis=1).astype(jnp.bfloat16)

    return lax.map(project, jnp.arange(NKB, dtype=jnp.int32)).reshape(TOKENS, D)
```

```python
import functools

import jax
import jax.numpy as jnp
from jax import lax
from jax.experimental import pallas as pl
from jax.experimental.pallas import tpu as pltpu
from jax.sharding import PartitionSpec as P

QH = 32
KVH = 8
HD = 128
BLOCK = 64
GROUP = QH // KVH
SPAN = 8
WIDE = SPAN * BLOCK

floor_score = -1e30
exp2_scale = HD ** (-0.5) * 1.4426950408889634


def plan(vert_cols, slash_off, doc_ids, context, blocks):
    query_block = context * blocks + jnp.arange(blocks, dtype=jnp.int32)
    query_doc = lax.dynamic_slice_in_dim(doc_ids, context * blocks, blocks, 0)
    doc_start = jnp.sum((doc_ids[None, :] < query_doc[:, None]).astype(jnp.int32), axis=1)
    at = query_block[None, :, None]
    start = doc_start[None, :, None]
    slash_key = at - slash_off[:, None, :]
    slash_live = slash_key >= start
    column = jnp.broadcast_to(
        (vert_cols // BLOCK)[:, None, :], (vert_cols.shape[0], blocks, vert_cols.shape[1])
    )
    on_slash = jnp.any((at - column)[..., None] == slash_off[:, None, None, :], axis=-1)
    column_live = (column < at) & jnp.logical_not(on_slash & (column >= start))
    diagonal = jnp.broadcast_to(at, slash_key.shape[:2] + (1,))
    ids = jnp.concatenate([diagonal, slash_key, column], axis=-1)
    live = jnp.concatenate([diagonal >= 0, slash_live, column_live], axis=-1)
    seats = -(-ids.shape[-1] // SPAN) * SPAN
    order = jnp.arange(ids.shape[-1])
    seat = jnp.sum(
        (live[..., None, :] & (order[None, :] < order[:, None])).astype(jnp.int32), axis=-1
    )
    count = jnp.sum(live.astype(jnp.int32), axis=-1)
    chosen = live[..., None, :] & (seat[..., None, :] == jnp.arange(seats)[:, None])
    packed = jnp.sum(jnp.where(chosen, ids[..., None, :], 0), axis=-1)
    packed = jnp.where(jnp.arange(seats) < count[..., None], packed, at)
    return packed.reshape(-1), count.reshape(-1), seats


def attend_kernel(blocks, seats, ids_ref, count_ref, q_ref, k_ref, v_ref, o_ref, s_ref):
    head = pl.program_id(0)

    def one(index, carry):
        pair = head * blocks + index
        count = count_ref[pair]
        chunks = (count + SPAN - 1) // SPAN
        rows = pl.ds(pl.multiple_of(index * BLOCK, BLOCK), BLOCK)
        q = jnp.concatenate([q_ref[rows, g * HD:(g + 1) * HD] for g in range(GROUP)], axis=0)

        def gathered(ref, chunk):
            parts = []
            for j in range(SPAN):
                where = ids_ref[pair * seats + chunk * SPAN + j]
                parts.append(ref[pl.ds(pl.multiple_of(where * BLOCK, BLOCK), BLOCK), :])
            return jnp.concatenate(parts, axis=0)

        def whole(number):
            most = None
            for chunk in range(number):
                s = lax.dot_general(
                    q, gathered(k_ref, chunk), (((1,), (1,)), ((), ())),
                    preferred_element_type=jnp.float32,
                )
                lane = lax.broadcasted_iota(jnp.int32, s.shape, 1)
                if chunk == 0:
                    row = lax.broadcasted_iota(jnp.int32, s.shape, 0) % BLOCK
                    s = jnp.where((lane > row) & (lane < BLOCK), floor_score, s)
                if chunk == number - 1:
                    s = jnp.where(lane < (count - chunk * SPAN) * BLOCK, s, floor_score)
                s_ref[:, chunk * WIDE:(chunk + 1) * WIDE] = s
                for part in range(0, WIDE, HD):
                    piece = s[:, part:part + HD]
                    most = piece if most is None else jnp.maximum(most, piece)
            top = jnp.max(most, axis=1, keepdims=True)
            summed = None
            total = None
            for chunk in range(number):
                s = s_ref[:, chunk * WIDE:(chunk + 1) * WIDE]
                p = jnp.exp2((s - top) * exp2_scale)
                for part in range(0, WIDE, HD):
                    piece = p[:, part:part + HD]
                    total = piece if total is None else total + piece
                out = jnp.dot(
                    p.astype(jnp.bfloat16), gathered(v_ref, chunk),
                    preferred_element_type=jnp.float32,
                )
                summed = out if summed is None else summed + out
            out = (summed / jnp.sum(total, axis=1, keepdims=True)).astype(jnp.bfloat16)
            for g in range(GROUP):
                o_ref[rows, g * HD:(g + 1) * HD] = out[g * BLOCK:(g + 1) * BLOCK]

        for number in range(1, seats // SPAN + 1):
            pl.when(chunks == number)(functools.partial(whole, number))
        return carry

    lax.fori_loop(0, blocks, one, 0)


def attend(query, keys, values, ids, count, seats):
    rows = query.shape[0]
    heads = keys.shape[1] // HD
    blocks = rows // BLOCK
    tokens = keys.shape[0]
    return pl.pallas_call(
        functools.partial(attend_kernel, blocks, seats),
        grid=(heads,),
        out_shape=jax.ShapeDtypeStruct(query.shape, jnp.bfloat16),
        in_specs=[
            pl.BlockSpec(memory_space=pltpu.SMEM),
            pl.BlockSpec(memory_space=pltpu.SMEM),
            pl.BlockSpec((rows, GROUP * HD), lambda h: (0, h)),
            pl.BlockSpec((tokens, HD), lambda h: (0, h)),
            pl.BlockSpec((tokens, HD), lambda h: (0, h)),
        ],
        out_specs=pl.BlockSpec((rows, GROUP * HD), lambda h: (0, h)),
        scratch_shapes=[pltpu.VMEM((GROUP * BLOCK, seats * BLOCK), jnp.float32)],
        compiler_params=pltpu.CompilerParams(vmem_limit_bytes=48 * 1024 * 1024),
        name="attend",
    )(ids, count, query, keys, values)


def per_device(query, keys, values, vert_cols, slash_off, doc_ids, out_weight):
    blocks = keys.shape[0] // BLOCK
    context = lax.axis_index("context")
    ids, count, seats = plan(vert_cols, slash_off, doc_ids, context, blocks)
    all_keys = lax.all_gather(keys, "context", axis=0, tiled=True)
    all_values = lax.all_gather(values, "context", axis=0, tiled=True)
    attended = attend(query, all_keys, all_values, ids, count, seats)
    return lax.psum_scatter(
        jnp.dot(attended, out_weight, preferred_element_type=jnp.float32).astype(jnp.bfloat16),
        "tensor",
        scatter_dimension=0,
        tiled=True,
    )


def solution(mesh):
    placed = (
        P("context", "tensor"),
        P("context", "tensor"),
        P("context", "tensor"),
        P("tensor", None),
        P("tensor", None),
        P(),
        P("tensor", None),
    )
    return jax.shard_map(
        per_device,
        mesh=mesh,
        in_specs=placed,
        out_specs=P(("context", "tensor"), None),
        check_vma=False,
    )
```

```python
import functools

import jax
import jax.numpy as jnp
from jax import lax
from jax.experimental import pallas as pl
from jax.experimental.pallas import tpu as pltpu
from jax.sharding import PartitionSpec as P

QH = 32
KVH = 8
HD = 128
BLOCK = 64
GROUP = QH // KVH
SPAN = 8
WIDE = SPAN * BLOCK

floor_score = -1e30
exp2_scale = HD ** (-0.5) * 1.4426950408889634


def plan(vert_cols, slash_off, doc_ids, context, blocks):
    query_block = context * blocks + jnp.arange(blocks, dtype=jnp.int32)
    query_doc = lax.dynamic_slice_in_dim(doc_ids, context * blocks, blocks, 0)
    doc_start = jnp.sum((doc_ids[None, :] < query_doc[:, None]).astype(jnp.int32), axis=1)
    at = query_block[None, :, None]
    start = doc_start[None, :, None]
    slash_key = at - slash_off[:, None, :]
    slash_live = slash_key >= start
    column = jnp.broadcast_to(
        (vert_cols // BLOCK)[:, None, :], (vert_cols.shape[0], blocks, vert_cols.shape[1])
    )
    on_slash = jnp.any((at - column)[..., None] == slash_off[:, None, None, :], axis=-1)
    column_live = (column < at) & jnp.logical_not(on_slash & (column >= start))
    diagonal = jnp.broadcast_to(at, slash_key.shape[:2] + (1,))
    ids = jnp.concatenate([diagonal, slash_key, column], axis=-1)
    live = jnp.concatenate([diagonal >= 0, slash_live, column_live], axis=-1)
    seats = -(-ids.shape[-1] // SPAN) * SPAN
    order = jnp.arange(ids.shape[-1])
    seat = jnp.sum(
        (live[..., None, :] & (order[None, :] < order[:, None])).astype(jnp.int32), axis=-1
    )
    count = jnp.sum(live.astype(jnp.int32), axis=-1)
    chosen = live[..., None, :] & (seat[..., None, :] == jnp.arange(seats)[:, None])
    packed = jnp.sum(jnp.where(chosen, ids[..., None, :], 0), axis=-1)
    packed = jnp.where(jnp.arange(seats) < count[..., None], packed, at)
    return packed.reshape(-1), count.reshape(-1), seats


def attend_kernel(blocks, here, seats, part_ref, ids_ref, count_ref, q_ref, k_ref, v_ref, o_ref, s_ref):
    head = pl.program_id(0)
    lead = part_ref[0] * here

    def one(index, carry):
        pair = head * blocks + lead + index
        count = count_ref[pair]
        chunks = (count + SPAN - 1) // SPAN
        rows = pl.ds(pl.multiple_of(index * BLOCK, BLOCK), BLOCK)
        q = jnp.concatenate([q_ref[rows, g * HD:(g + 1) * HD] for g in range(GROUP)], axis=0)

        def gathered(ref, chunk):
            parts = []
            for j in range(SPAN):
                where = ids_ref[pair * seats + chunk * SPAN + j]
                parts.append(ref[pl.ds(pl.multiple_of(where * BLOCK, BLOCK), BLOCK), :])
            return jnp.concatenate(parts, axis=0)

        def whole(number):
            most = None
            for chunk in range(number):
                s = lax.dot_general(
                    q, gathered(k_ref, chunk), (((1,), (1,)), ((), ())),
                    preferred_element_type=jnp.float32,
                )
                lane = lax.broadcasted_iota(jnp.int32, s.shape, 1)
                if chunk == 0:
                    row = lax.broadcasted_iota(jnp.int32, s.shape, 0) % BLOCK
                    s = jnp.where((lane > row) & (lane < BLOCK), floor_score, s)
                if chunk == number - 1:
                    s = jnp.where(lane < (count - chunk * SPAN) * BLOCK, s, floor_score)
                s_ref[:, chunk * WIDE:(chunk + 1) * WIDE] = s
                for part in range(0, WIDE, HD):
                    piece = s[:, part:part + HD]
                    most = piece if most is None else jnp.maximum(most, piece)
            top = jnp.max(most, axis=1, keepdims=True)
            summed = None
            total = None
            for chunk in range(number):
                s = s_ref[:, chunk * WIDE:(chunk + 1) * WIDE]
                p = jnp.exp2((s - top) * exp2_scale)
                for part in range(0, WIDE, HD):
                    piece = p[:, part:part + HD]
                    total = piece if total is None else total + piece
                out = jnp.dot(
                    p.astype(jnp.bfloat16), gathered(v_ref, chunk),
                    preferred_element_type=jnp.float32,
                )
                summed = out if summed is None else summed + out
            out = (summed / jnp.sum(total, axis=1, keepdims=True)).astype(jnp.bfloat16)
            for g in range(GROUP):
                o_ref[rows, g * HD:(g + 1) * HD] = out[g * BLOCK:(g + 1) * BLOCK]

        for number in range(1, seats // SPAN + 1):
            pl.when(chunks == number)(functools.partial(whole, number))
        return carry

    lax.fori_loop(0, here, one, 0)


def attend(query, keys, values, part, parts, ids, count, seats):
    rows = query.shape[0] // parts
    heads = keys.shape[1] // HD
    tokens = keys.shape[0]
    grid_spec = pltpu.PrefetchScalarGridSpec(
        num_scalar_prefetch=3,
        grid=(heads,),
        in_specs=[
            pl.BlockSpec((rows, GROUP * HD), lambda h, part_ref, *_: (part_ref[0], h)),
            pl.BlockSpec((tokens, HD), lambda h, *_: (0, h)),
            pl.BlockSpec((tokens, HD), lambda h, *_: (0, h)),
        ],
        out_specs=pl.BlockSpec((rows, GROUP * HD), lambda h, *_: (0, h)),
        scratch_shapes=[pltpu.VMEM((GROUP * BLOCK, seats * BLOCK), jnp.float32)],
    )
    pairs = heads * rows * GROUP
    return pl.pallas_call(
        functools.partial(attend_kernel, query.shape[0] // BLOCK, rows // BLOCK, seats),
        grid_spec=grid_spec,
        out_shape=jax.ShapeDtypeStruct((rows, query.shape[1]), jnp.bfloat16),
        compiler_params=pltpu.CompilerParams(vmem_limit_bytes=48 * 1024 * 1024),
        cost_estimate=pl.CostEstimate(
            flops=4 * pairs * seats * BLOCK * HD,
            bytes_accessed=4 * tokens * heads * HD,
            transcendentals=pairs * seats * BLOCK,
        ),
        name="attend",
    )(part.reshape(1), ids, count, query, keys, values)


LEVEL = 4


def gather_kernel(levels, k_ref, v_ref, gk_ref, gv_ref, send_sem, recv_sem, own_sem):
    rows = k_ref.shape[0]
    me = lax.axis_index("context")
    level = me // LEVEL
    side = (me // 2) % 2
    core = me % 2
    over = me + 2 - 4 * side
    twin = me + 1 - 2 * core
    last = level == levels - 1

    barrier = pltpu.get_barrier_semaphore()

    def greet(device):
        pl.semaphore_signal(
            barrier, inc=1, device_id={"context": device}, device_id_type=pl.DeviceIdType.MESH
        )

    greet(over)
    greet(twin)
    pl.when(level > 0)(lambda: greet(me - LEVEL))
    pl.when(level < levels - 1)(lambda: greet(me + LEVEL))
    pl.semaphore_wait(
        barrier, 2 + jnp.where(level > 0, 1, 0) + jnp.where(level < levels - 1, 1, 0)
    )

    inputs, gathered = (k_ref, v_ref), (gk_ref, gv_ref)

    def place(owner, part):
        return gathered[part].at[pl.ds(pl.multiple_of(owner * rows, rows), rows), :]

    def copy(owner, part, device, sem, own=False):
        return pltpu.make_async_remote_copy(
            src_ref=inputs[part] if own else place(owner, part),
            dst_ref=place(owner, part),
            send_sem=send_sem.at[sem],
            recv_sem=recv_sem.at[owner, part],
            device_id={"context": device},
            device_id_type=pl.DeviceIdType.MESH,
        )

    def sem_of(kind, step, part):
        return (kind * levels + step) * 2 + part

    sent = []

    def send(condition, *args, **kwargs):
        pl.when(condition)(lambda: copy(*args, **kwargs).start())
        sent.append((condition, args, kwargs))

    def arrive(condition, owner, part):
        pl.when(condition)(lambda: copy(owner, part, twin, 0).wait_recv())

    own_copies = [
        pltpu.make_async_copy(inputs[part], place(me, part), own_sem.at[part]) for part in range(2)
    ]
    for own_copy in own_copies:
        own_copy.start()

    climber = core
    for step in range(levels + 1):
        from_level = level - step
        if step < levels:
            held = from_level >= 0
            owner = from_level * LEVEL + side * 2 + core
            for part in range(2):
                if step:
                    arrive(held, owner, part)
                send(held & (level < levels - 1), owner, part, me + LEVEL, sem_of(0, step, part), own=step == 0)
                crosses = held & (side == 0) if step == 0 else held
                if part == 0 and step > 0:
                    crosses = crosses & jnp.logical_not((from_level == 0) & (side == 0))
                send(crosses, owner, part, over, sem_of(1, step, part), own=step == 0)
                send(held & (core == 0) if step == 0 else held, owner, part, twin, sem_of(2, step, part), own=step == 0)
        if step:
            back = step - 1
            before = level - back
            owner = before * LEVEL + (1 - side) * 2 + core
            for part in range(2):
                crossed = (before >= 0) & (side == 1) if back == 0 else before >= 0
                arrive(crossed, owner, part)
                if part == 0:
                    climbs = crossed & (before == 0) & (side == 1)
                    send(climbs & (level < levels - 1), owner, part, me + LEVEL, sem_of(4, back, part))
                send(crossed, owner, part, twin, sem_of(3, back, part))
    for before in range(levels):
        for other in range(2):
            for part in range(2):
                owner = before * LEVEL + other * 2 + 1 - core
                mine = (before == level) & ((other < side) | ((other == side) & (core == 1)))
                arrive((before < level) | mine, owner, part)
    for condition, args, kwargs in sent:
        pl.when(condition)(lambda args=args, kwargs=kwargs: copy(*args, **kwargs).wait_send())
    for own_copy in own_copies:
        own_copy.wait()


def gather(keys, values, count):
    levels = count // LEVEL
    shape = jax.ShapeDtypeStruct((count * keys.shape[0], keys.shape[1]), keys.dtype)
    return pl.pallas_call(
        functools.partial(gather_kernel, levels),
        out_shape=(shape, shape),
        in_specs=[pl.BlockSpec(memory_space=pl.ANY)] * 2,
        out_specs=(pl.BlockSpec(memory_space=pl.ANY),) * 2,
        scratch_shapes=[
            pltpu.SemaphoreType.DMA((5 * levels * 2,)),
            pltpu.SemaphoreType.DMA((count, 2)),
            pltpu.SemaphoreType.DMA((2,)),
        ],
        compiler_params=pltpu.CompilerParams(collective_id=0, has_side_effects=True),
        name="gather",
    )(keys, values)


def per_device(query, keys, values, vert_cols, slash_off, doc_ids, out_weight):
    blocks = keys.shape[0] // BLOCK
    context = lax.axis_index("context")
    tensor = lax.axis_index("tensor")
    shares = lax.axis_size("tensor")
    ids, count, seats = plan(vert_cols, slash_off, doc_ids, context, blocks)
    all_keys, all_values = gather(keys, values, lax.axis_size("context"))

    def projected(rows, weight):
        return jnp.dot(rows, weight, preferred_element_type=jnp.float32).astype(jnp.bfloat16)

    if shares != 2 or blocks % shares:
        first = jnp.zeros((), jnp.int32)
        rows = attend(query, all_keys, all_values, first, 1, ids, count, seats)
        return lax.psum_scatter(
            projected(rows, out_weight), "tensor", scatter_dimension=0, tiled=True
        )
    theirs = attend(query, all_keys, all_values, 1 - tensor, shares, ids, count, seats)
    cuts = 2
    width = out_weight.shape[1] // cuts
    moved = []
    for cut in range(cuts):
        weight = out_weight[:, cut * width:(cut + 1) * width]
        moved.append(lax.ppermute(projected(theirs, weight), "tensor", [(0, 1), (1, 0)]))
    part, _ = lax.optimization_barrier((tensor, theirs))
    mine = attend(query, all_keys, all_values, part, shares, ids, count, seats)
    outs = []
    for cut in range(cuts):
        weight = out_weight[:, cut * width:(cut + 1) * width]
        outs.append(projected(mine, weight).astype(jnp.float32) + moved[cut].astype(jnp.float32))
    return jnp.concatenate(outs, axis=1).astype(jnp.bfloat16)


def solution(mesh):
    placed = (
        P("context", "tensor"),
        P("context", "tensor"),
        P("context", "tensor"),
        P("tensor", None),
        P("tensor", None),
        P(),
        P("tensor", None),
    )
    return jax.shard_map(
        per_device,
        mesh=mesh,
        in_specs=placed,
        out_specs=P(("context", "tensor"), None),
        check_vma=False,
    )
```

```python
import functools

import jax
import jax.numpy as jnp
from jax import lax
from jax.experimental import pallas as pl
from jax.experimental.pallas import tpu as pltpu
from jax.sharding import PartitionSpec as P

QH = 32
KVH = 8
HD = 128
BLOCK = 64
GROUP = QH // KVH
SPAN = 8
WIDE = SPAN * BLOCK

floor_score = -1e30
exp2_scale = HD ** (-0.5) * 1.4426950408889634


def attend_kernel(
    here, seats, at_ref, column_ref, slash_ref, doc_ref, q_ref, k_ref, v_ref, o_ref, s_ref, ids_ref, mark_ref
):
    head = pl.program_id(0)
    heads = pl.num_programs(0)
    columns = column_ref.shape[0] // heads
    slashes = slash_ref.shape[0] // heads
    lead = at_ref[1]
    spare = doc_ref.shape[0]

    @pl.when(head == 0)
    def _():
        def clear(index, carry):
            mark_ref[index] = -1
            return carry

        lax.fori_loop(0, spare + 1, clear, 0)

    def one(index, carry):
        pair = head * here + index
        block = lead + index
        doc = doc_ref[block]
        ids_ref[0] = block
        count = jnp.int32(1)
        for j in range(slashes):
            key = block - slash_ref[head * slashes + j]
            live = (key >= 0) & (doc_ref[jnp.maximum(key, 0)] == doc)
            ids_ref[count] = key
            mark_ref[jnp.where(live, key, spare)] = pair
            count = count + jnp.where(live, 1, 0)
        for j in range(columns):
            key = column_ref[head * columns + j] // BLOCK
            live = (key < block) & (mark_ref[key] != pair)
            ids_ref[count] = key
            count = count + jnp.where(live, 1, 0)
        for j in range(SPAN):
            ids_ref[count + j] = block
        chunks = (count + SPAN - 1) // SPAN
        rows = pl.ds(pl.multiple_of(index * BLOCK, BLOCK), BLOCK)
        q = jnp.concatenate([q_ref[rows, g * HD:(g + 1) * HD] for g in range(GROUP)], axis=0)

        def gathered(ref, chunk):
            parts = []
            for j in range(SPAN):
                where = ids_ref[chunk * SPAN + j]
                parts.append(ref[pl.ds(pl.multiple_of(where * BLOCK, BLOCK), BLOCK), :])
            return jnp.concatenate(parts, axis=0)

        def whole(number):
            most = None
            for chunk in range(number):
                s = lax.dot_general(
                    q, gathered(k_ref, chunk), (((1,), (1,)), ((), ())),
                    preferred_element_type=jnp.float32,
                )
                lane = lax.broadcasted_iota(jnp.int32, s.shape, 1)
                if chunk == 0:
                    row = lax.broadcasted_iota(jnp.int32, s.shape, 0) % BLOCK
                    s = jnp.where((lane > row) & (lane < BLOCK), floor_score, s)
                if chunk == number - 1:
                    s = jnp.where(lane < (count - chunk * SPAN) * BLOCK, s, floor_score)
                s_ref[:, chunk * WIDE:(chunk + 1) * WIDE] = s
                for part in range(0, WIDE, HD):
                    piece = s[:, part:part + HD]
                    most = piece if most is None else jnp.maximum(most, piece)
            top = jnp.max(most, axis=1, keepdims=True)
            summed = None
            total = None
            for chunk in range(number):
                s = s_ref[:, chunk * WIDE:(chunk + 1) * WIDE]
                p = jnp.exp2((s - top) * exp2_scale)
                for part in range(0, WIDE, HD):
                    piece = p[:, part:part + HD]
                    total = piece if total is None else total + piece
                out = jnp.dot(
                    p.astype(jnp.bfloat16), gathered(v_ref, chunk),
                    preferred_element_type=jnp.float32,
                )
                summed = out if summed is None else summed + out
            out = (summed / jnp.sum(total, axis=1, keepdims=True)).astype(jnp.bfloat16)
            for g in range(GROUP):
                o_ref[rows, g * HD:(g + 1) * HD] = out[g * BLOCK:(g + 1) * BLOCK]

        for number in range(1, seats // SPAN + 1):
            pl.when(chunks == number)(functools.partial(whole, number))
        return carry

    lax.fori_loop(0, here, one, 0)


def attend(query, keys, values, part, parts, first_block, vert_cols, slash_off, doc_ids):
    rows = query.shape[0] // parts
    heads = keys.shape[1] // HD
    tokens = keys.shape[0]
    most = 1 + vert_cols.shape[1] + slash_off.shape[1]
    seats = -(-most // SPAN) * SPAN
    grid_spec = pltpu.PrefetchScalarGridSpec(
        num_scalar_prefetch=4,
        grid=(heads,),
        in_specs=[
            pl.BlockSpec((rows, GROUP * HD), lambda h, at_ref, *_: (at_ref[0], h)),
            pl.BlockSpec((tokens, HD), lambda h, *_: (0, h)),
            pl.BlockSpec((tokens, HD), lambda h, *_: (0, h)),
        ],
        out_specs=pl.BlockSpec((rows, GROUP * HD), lambda h, *_: (0, h)),
        scratch_shapes=[
            pltpu.VMEM((GROUP * BLOCK, seats * BLOCK), jnp.float32),
            pltpu.SMEM((seats + SPAN,), jnp.int32),
            pltpu.SMEM((doc_ids.shape[0] + 1,), jnp.int32),
        ],
    )
    pairs = heads * rows * GROUP
    at = jnp.stack([part, first_block + part * (rows // BLOCK)])
    return pl.pallas_call(
        functools.partial(attend_kernel, rows // BLOCK, seats),
        grid_spec=grid_spec,
        out_shape=jax.ShapeDtypeStruct((rows, query.shape[1]), jnp.bfloat16),
        compiler_params=pltpu.CompilerParams(vmem_limit_bytes=48 * 1024 * 1024),
        cost_estimate=pl.CostEstimate(
            flops=4 * pairs * seats * BLOCK * HD,
            bytes_accessed=4 * tokens * heads * HD,
            transcendentals=pairs * seats * BLOCK,
        ),
        name="attend",
    )(at, vert_cols.reshape(-1), slash_off.reshape(-1), doc_ids, query, keys, values)


def combine_kernel(own_ref, *refs):
    width = refs[0].shape[1]
    for cut, moved_ref in enumerate(refs[:-1]):
        where = slice(cut * width, (cut + 1) * width)
        total = own_ref[:, where].astype(jnp.float32) + moved_ref[...].astype(jnp.float32)
        refs[-1][:, where] = total.astype(jnp.bfloat16)


def combine(own, moved):
    step = 32
    width = moved[0].shape[1]
    return pl.pallas_call(
        combine_kernel,
        grid=(own.shape[0] // step,),
        out_shape=jax.ShapeDtypeStruct(own.shape, own.dtype),
        in_specs=[pl.BlockSpec((step, own.shape[1]), lambda i: (i, 0))]
        + [pl.BlockSpec((step, width), lambda i: (i, 0))] * len(moved),
        out_specs=pl.BlockSpec((step, own.shape[1]), lambda i: (i, 0)),
        name="combine",
    )(own, *moved)


LEVEL = 4


def gather_kernel(levels, k_ref, v_ref, gk_ref, gv_ref, send_sem, recv_sem, own_sem):
    rows = k_ref.shape[0]
    me = lax.axis_index("context")
    level = me // LEVEL
    side = (me // 2) % 2
    core = me % 2
    over = me + 2 - 4 * side
    twin = me + 1 - 2 * core
    last = level == levels - 1

    barrier = pltpu.get_barrier_semaphore()

    def greet(device):
        pl.semaphore_signal(
            barrier, inc=1, device_id={"context": device}, device_id_type=pl.DeviceIdType.MESH
        )

    greet(over)
    greet(twin)
    pl.when(level > 0)(lambda: greet(me - LEVEL))
    pl.when(level < levels - 1)(lambda: greet(me + LEVEL))
    pl.semaphore_wait(
        barrier, 2 + jnp.where(level > 0, 1, 0) + jnp.where(level < levels - 1, 1, 0)
    )

    inputs, gathered = (k_ref, v_ref), (gk_ref, gv_ref)

    def place(owner, part):
        return gathered[part].at[pl.ds(pl.multiple_of(owner * rows, rows), rows), :]

    def copy(owner, part, device, sem, own=False):
        return pltpu.make_async_remote_copy(
            src_ref=inputs[part] if own else place(owner, part),
            dst_ref=place(owner, part),
            send_sem=send_sem.at[sem],
            recv_sem=recv_sem.at[owner, part],
            device_id={"context": device},
            device_id_type=pl.DeviceIdType.MESH,
        )

    def sem_of(kind, step, part):
        return (kind * levels + step) * 2 + part

    sent = []

    def send(condition, *args, **kwargs):
        pl.when(condition)(lambda: copy(*args, **kwargs).start())
        sent.append((condition, args, kwargs))

    def arrive(condition, owner, part):
        pl.when(condition)(lambda: copy(owner, part, twin, 0).wait_recv())

    own_copies = [
        pltpu.make_async_copy(inputs[part], place(me, part), own_sem.at[part]) for part in range(2)
    ]
    for own_copy in own_copies:
        own_copy.start()

    climber = core
    for step in range(levels + 1):
        from_level = level - step
        if step < levels:
            held = from_level >= 0
            owner = from_level * LEVEL + side * 2 + core
            for part in range(2):
                if step:
                    arrive(held, owner, part)
                send(held & (level < levels - 1), owner, part, me + LEVEL, sem_of(0, step, part), own=step == 0)
                crosses = held & (side == 0) if step == 0 else held
                if part == 0 and step > 0:
                    crosses = crosses & jnp.logical_not((from_level == 0) & (side == 0))
                send(crosses, owner, part, over, sem_of(1, step, part), own=step == 0)
                send(held & (core == 0) if step == 0 else held, owner, part, twin, sem_of(2, step, part), own=step == 0)
        if step:
            back = step - 1
            before = level - back
            owner = before * LEVEL + (1 - side) * 2 + core
            for part in range(2):
                crossed = (before >= 0) & (side == 1) if back == 0 else before >= 0
                arrive(crossed, owner, part)
                if part == 0:
                    climbs = crossed & (before == 0) & (side == 1)
                    send(climbs & (level < levels - 1), owner, part, me + LEVEL, sem_of(4, back, part))
                send(crossed, owner, part, twin, sem_of(3, back, part))
    for before in range(levels):
        for other in range(2):
            for part in range(2):
                owner = before * LEVEL + other * 2 + 1 - core
                mine = (before == level) & ((other < side) | ((other == side) & (core == 1)))
                arrive((before < level) | mine, owner, part)
    for condition, args, kwargs in sent:
        pl.when(condition)(lambda args=args, kwargs=kwargs: copy(*args, **kwargs).wait_send())
    for own_copy in own_copies:
        own_copy.wait()


def gather(keys, values, count):
    levels = count // LEVEL
    shape = jax.ShapeDtypeStruct((count * keys.shape[0], keys.shape[1]), keys.dtype)
    return pl.pallas_call(
        functools.partial(gather_kernel, levels),
        out_shape=(shape, shape),
        in_specs=[pl.BlockSpec(memory_space=pl.ANY)] * 2,
        out_specs=(pl.BlockSpec(memory_space=pl.ANY),) * 2,
        scratch_shapes=[
            pltpu.SemaphoreType.DMA((5 * levels * 2,)),
            pltpu.SemaphoreType.DMA((count, 2)),
            pltpu.SemaphoreType.DMA((2,)),
        ],
        compiler_params=pltpu.CompilerParams(collective_id=0, has_side_effects=True),
        name="gather",
    )(keys, values)


def per_device(query, keys, values, vert_cols, slash_off, doc_ids, out_weight):
    blocks = keys.shape[0] // BLOCK
    context = lax.axis_index("context")
    tensor = lax.axis_index("tensor")
    shares = lax.axis_size("tensor")
    all_keys, all_values = gather(keys, values, lax.axis_size("context"))

    def attended(part, parts):
        return attend(
            query, all_keys, all_values, part, parts, context * blocks, vert_cols, slash_off, doc_ids
        )

    def projected(rows, weight):
        return jnp.dot(rows, weight, preferred_element_type=jnp.float32).astype(jnp.bfloat16)

    if shares != 2 or blocks % shares:
        return lax.psum_scatter(
            projected(attended(jnp.zeros((), jnp.int32), 1), out_weight),
            "tensor",
            scatter_dimension=0,
            tiled=True,
        )
    theirs = attended(1 - tensor, shares)
    cuts = 4
    width = out_weight.shape[1] // cuts
    moved = []
    for cut in range(cuts):
        weight = out_weight[:, cut * width:(cut + 1) * width]
        moved.append(lax.ppermute(projected(theirs, weight), "tensor", [(0, 1), (1, 0)]))
    part, _ = lax.optimization_barrier((tensor, theirs))
    own = projected(attended(part, shares), out_weight)
    return combine(own, moved)


def solution(mesh):
    placed = (
        P("context", "tensor"),
        P("context", "tensor"),
        P("context", "tensor"),
        P("tensor", None),
        P("tensor", None),
        P(),
        P("tensor", None),
    )
    return jax.shard_map(
        per_device,
        mesh=mesh,
        in_specs=placed,
        out_specs=P(("context", "tensor"), None),
        check_vma=False,
    )
```

```python
import functools

import jax
import jax.numpy as jnp
from jax import lax
from jax.experimental import pallas as pl
from jax.experimental.pallas import tpu as pltpu
from jax.sharding import PartitionSpec as P

QH = 32
KVH = 8
HD = 128
BLOCK = 64
GROUP = QH // KVH
SPAN = 8
WIDE = SPAN * BLOCK

floor_score = -1e30
exp2_scale = HD ** (-0.5) * 1.4426950408889634


def attend_kernel(
    here, seats, at_ref, column_ref, slash_ref, doc_ref, q_ref, k_ref, v_ref, o_ref,
    s_ref, ids_ref, next_ref, mark_ref,
):
    head = pl.program_id(0)
    heads = pl.num_programs(0)
    columns = column_ref.shape[0] // heads
    slashes = slash_ref.shape[0] // heads
    lead = at_ref[1]
    spare = doc_ref.shape[0]
    tally = seats + SPAN

    def listed(pair):
        its_head = pair // here
        block = lead + pair % here
        doc = doc_ref[block]
        keys = [block - slash_ref[its_head * slashes + j] for j in range(slashes)]
        lives = [(key >= 0) & (doc_ref[jnp.maximum(key, 0)] == doc) for key in keys]
        for key, live in zip(keys, lives):
            mark_ref[jnp.where(live, key, spare)] = pair
        for j in range(columns):
            key = column_ref[its_head * columns + j] // BLOCK
            keys.append(key)
            lives.append((key < block) & (mark_ref[key] != pair))
        next_ref[0] = block
        count = jnp.int32(1)
        for key, live in zip(keys, lives):
            next_ref[count] = key
            count = count + jnp.where(live, 1, 0)
        for j in range(SPAN):
            next_ref[count + j] = block
        next_ref[tally] = count

    @pl.when(head == 0)
    def _():
        def clear(index, carry):
            mark_ref[index] = -1
            return carry

        lax.fori_loop(0, spare + 1, clear, 0)
        listed(jnp.int32(0))

    def one(index, carry):
        pair = head * here + index
        count = next_ref[tally]
        for j in range(seats):
            ids_ref[j] = next_ref[j]
        chunks = (count + SPAN - 1) // SPAN
        rows = pl.ds(pl.multiple_of(index * BLOCK, BLOCK), BLOCK)
        q = jnp.concatenate([q_ref[rows, g * HD:(g + 1) * HD] for g in range(GROUP)], axis=0)

        def gathered(ref, chunk):
            parts = []
            for j in range(SPAN):
                where = ids_ref[chunk * SPAN + j]
                parts.append(ref[pl.ds(pl.multiple_of(where * BLOCK, BLOCK), BLOCK), :])
            return jnp.concatenate(parts, axis=0)

        def whole(number):
            listed(jnp.minimum(pair + 1, heads * here - 1))
            most = None
            for chunk in range(number):
                s = lax.dot_general(
                    q, gathered(k_ref, chunk), (((1,), (1,)), ((), ())),
                    preferred_element_type=jnp.float32,
                )
                lane = lax.broadcasted_iota(jnp.int32, s.shape, 1)
                if chunk == 0:
                    row = lax.broadcasted_iota(jnp.int32, s.shape, 0) % BLOCK
                    s = jnp.where((lane > row) & (lane < BLOCK), floor_score, s)
                if chunk == number - 1:
                    s = jnp.where(lane < (count - chunk * SPAN) * BLOCK, s, floor_score)
                s_ref[:, chunk * WIDE:(chunk + 1) * WIDE] = s
                for part in range(0, WIDE, HD):
                    piece = s[:, part:part + HD]
                    most = piece if most is None else jnp.maximum(most, piece)
            top = jnp.max(most, axis=1, keepdims=True)
            summed = None
            total = None
            for chunk in range(number):
                s = s_ref[:, chunk * WIDE:(chunk + 1) * WIDE]
                p = jnp.exp2((s - top) * exp2_scale)
                for part in range(0, WIDE, HD):
                    piece = p[:, part:part + HD]
                    total = piece if total is None else total + piece
                out = jnp.dot(
                    p.astype(jnp.bfloat16), gathered(v_ref, chunk),
                    preferred_element_type=jnp.float32,
                )
                summed = out if summed is None else summed + out
            out = (summed / jnp.sum(total, axis=1, keepdims=True)).astype(jnp.bfloat16)
            for g in range(GROUP):
                o_ref[rows, g * HD:(g + 1) * HD] = out[g * BLOCK:(g + 1) * BLOCK]

        for number in range(1, seats // SPAN + 1):
            pl.when(chunks == number)(functools.partial(whole, number))
        return carry

    lax.fori_loop(0, here, one, 0)


def attend(query, keys, values, part, parts, first_block, vert_cols, slash_off, doc_ids):
    rows = query.shape[0] // parts
    heads = keys.shape[1] // HD
    tokens = keys.shape[0]
    most = 1 + vert_cols.shape[1] + slash_off.shape[1]
    seats = -(-most // SPAN) * SPAN
    grid_spec = pltpu.PrefetchScalarGridSpec(
        num_scalar_prefetch=4,
        grid=(heads,),
        in_specs=[
            pl.BlockSpec((rows, GROUP * HD), lambda h, at_ref, *_: (at_ref[0], h)),
            pl.BlockSpec((tokens, HD), lambda h, *_: (0, h)),
            pl.BlockSpec((tokens, HD), lambda h, *_: (0, h)),
        ],
        out_specs=pl.BlockSpec((rows, GROUP * HD), lambda h, *_: (0, h)),
        scratch_shapes=[
            pltpu.VMEM((GROUP * BLOCK, seats * BLOCK), jnp.float32),
            pltpu.SMEM((seats,), jnp.int32),
            pltpu.SMEM((seats + SPAN + 1,), jnp.int32),
            pltpu.SMEM((doc_ids.shape[0] + 1,), jnp.int32),
        ],
    )
    pairs = heads * rows * GROUP
    at = jnp.stack([part, first_block + part * (rows // BLOCK)])
    return pl.pallas_call(
        functools.partial(attend_kernel, rows // BLOCK, seats),
        grid_spec=grid_spec,
        out_shape=jax.ShapeDtypeStruct((rows, query.shape[1]), jnp.bfloat16),
        compiler_params=pltpu.CompilerParams(vmem_limit_bytes=48 * 1024 * 1024),
        cost_estimate=pl.CostEstimate(
            flops=4 * pairs * seats * BLOCK * HD,
            bytes_accessed=4 * tokens * heads * HD,
            transcendentals=pairs * seats * BLOCK,
        ),
        name="attend",
    )(at, vert_cols.reshape(-1), slash_off.reshape(-1), doc_ids, query, keys, values)


TILE = 512


def project_kernel(adds, rows_ref, weight_ref, *refs):
    part = jnp.dot(rows_ref[...], weight_ref[...], preferred_element_type=jnp.float32)
    part = part.astype(jnp.bfloat16)
    if adds:
        part = (part.astype(jnp.float32) + refs[0][...].astype(jnp.float32)).astype(jnp.bfloat16)
    refs[-1][...] = part


def project(rows, weight, cut, cuts, moved=None, into=None):
    height, depth = rows.shape
    columns = weight.shape[1]
    steps = columns // cuts // TILE
    lead = cut * steps
    args = [rows, weight]
    in_specs = [
        pl.BlockSpec((height, depth), lambda i: (0, 0)),
        pl.BlockSpec((depth, TILE), lambda i: (0, lead + i)),
    ]
    aliases = {}
    if moved is None:
        shape = (height, columns // cuts)
        out_spec = pl.BlockSpec((height, TILE), lambda i: (0, i))
    else:
        shape = (height, columns)
        out_spec = pl.BlockSpec((height, TILE), lambda i: (0, lead + i))
        args.append(moved)
        in_specs.append(pl.BlockSpec((height, TILE), lambda i: (0, i)))
        if into is not None:
            aliases = {len(args): 0}
            args.append(into)
            in_specs.append(pl.BlockSpec(memory_space=pl.ANY))
    return pl.pallas_call(
        functools.partial(project_kernel, moved is not None),
        grid=(steps,),
        out_shape=jax.ShapeDtypeStruct(shape, rows.dtype),
        in_specs=in_specs,
        out_specs=out_spec,
        input_output_aliases=aliases,
        compiler_params=pltpu.CompilerParams(vmem_limit_bytes=48 * 1024 * 1024),
        cost_estimate=pl.CostEstimate(
            flops=2 * height * depth * columns // cuts,
            bytes_accessed=2 * depth * columns // cuts,
            transcendentals=0,
        ),
        name="project",
    )(*args)


LEVEL = 4


def gather_kernel(levels, k_ref, v_ref, gk_ref, gv_ref, send_sem, recv_sem, own_sem):
    rows = k_ref.shape[0]
    me = lax.axis_index("context")
    level = me // LEVEL
    side = (me // 2) % 2
    core = me % 2
    over = me + 2 - 4 * side
    twin = me + 1 - 2 * core
    last = level == levels - 1

    barrier = pltpu.get_barrier_semaphore()

    def greet(device):
        pl.semaphore_signal(
            barrier, inc=1, device_id={"context": device}, device_id_type=pl.DeviceIdType.MESH
        )

    greet(over)
    greet(twin)
    pl.when(level > 0)(lambda: greet(me - LEVEL))
    pl.when(level < levels - 1)(lambda: greet(me + LEVEL))
    pl.semaphore_wait(
        barrier, 2 + jnp.where(level > 0, 1, 0) + jnp.where(level < levels - 1, 1, 0)
    )

    inputs, gathered = (k_ref, v_ref), (gk_ref, gv_ref)

    def place(owner, part):
        return gathered[part].at[pl.ds(pl.multiple_of(owner * rows, rows), rows), :]

    def copy(owner, part, device, sem, own=False):
        return pltpu.make_async_remote_copy(
            src_ref=inputs[part] if own else place(owner, part),
            dst_ref=place(owner, part),
            send_sem=send_sem.at[sem],
            recv_sem=recv_sem.at[owner, part],
            device_id={"context": device},
            device_id_type=pl.DeviceIdType.MESH,
        )

    def sem_of(kind, step, part):
        return (kind * levels + step) * 2 + part

    sent = []

    def send(condition, *args, **kwargs):
        pl.when(condition)(lambda: copy(*args, **kwargs).start())
        sent.append((condition, args, kwargs))

    def arrive(condition, owner, part):
        pl.when(condition)(lambda: copy(owner, part, twin, 0).wait_recv())

    own_copies = [
        pltpu.make_async_copy(inputs[part], place(me, part), own_sem.at[part]) for part in range(2)
    ]
    for own_copy in own_copies:
        own_copy.start()

    climber = core
    for step in range(levels + 1):
        from_level = level - step
        if step < levels:
            held = from_level >= 0
            owner = from_level * LEVEL + side * 2 + core
            for part in range(2):
                if step:
                    arrive(held, owner, part)
                send(held & (level < levels - 1), owner, part, me + LEVEL, sem_of(0, step, part), own=step == 0)
                crosses = held & (side == 0) if step == 0 else held
                if part == 0 and step > 0:
                    crosses = crosses & jnp.logical_not((from_level == 0) & (side == 0))
                send(crosses, owner, part, over, sem_of(1, step, part), own=step == 0)
                send(held & (core == 0) if step == 0 else held, owner, part, twin, sem_of(2, step, part), own=step == 0)
        if step:
            back = step - 1
            before = level - back
            owner = before * LEVEL + (1 - side) * 2 + core
            for part in range(2):
                crossed = (before >= 0) & (side == 1) if back == 0 else before >= 0
                arrive(crossed, owner, part)
                if part == 0:
                    climbs = crossed & (before == 0) & (side == 1)
                    send(climbs & (level < levels - 1), owner, part, me + LEVEL, sem_of(4, back, part))
                send(crossed, owner, part, twin, sem_of(3, back, part))
    for before in range(levels):
        for other in range(2):
            for part in range(2):
                owner = before * LEVEL + other * 2 + 1 - core
                mine = (before == level) & ((other < side) | ((other == side) & (core == 1)))
                arrive((before < level) | mine, owner, part)
    for condition, args, kwargs in sent:
        pl.when(condition)(lambda args=args, kwargs=kwargs: copy(*args, **kwargs).wait_send())
    for own_copy in own_copies:
        own_copy.wait()


def gather(keys, values, count):
    levels = count // LEVEL
    shape = jax.ShapeDtypeStruct((count * keys.shape[0], keys.shape[1]), keys.dtype)
    return pl.pallas_call(
        functools.partial(gather_kernel, levels),
        out_shape=(shape, shape),
        in_specs=[pl.BlockSpec(memory_space=pl.ANY)] * 2,
        out_specs=(pl.BlockSpec(memory_space=pl.ANY),) * 2,
        scratch_shapes=[
            pltpu.SemaphoreType.DMA((5 * levels * 2,)),
            pltpu.SemaphoreType.DMA((count, 2)),
            pltpu.SemaphoreType.DMA((2,)),
        ],
        compiler_params=pltpu.CompilerParams(
            collective_id=0, has_side_effects=True, vmem_limit_bytes=60 * 1024 * 1024
        ),
        name="gather",
    )(keys, values)


def per_device(query, keys, values, vert_cols, slash_off, doc_ids, out_weight):
    blocks = keys.shape[0] // BLOCK
    context = lax.axis_index("context")
    tensor = lax.axis_index("tensor")
    shares = lax.axis_size("tensor")
    all_keys, all_values = gather(keys, values, lax.axis_size("context"))

    def attended(part, parts):
        return attend(
            query, all_keys, all_values, part, parts, context * blocks, vert_cols, slash_off, doc_ids
        )

    def projected(rows, weight):
        return jnp.dot(rows, weight, preferred_element_type=jnp.float32).astype(jnp.bfloat16)

    if shares != 2 or blocks % shares:
        return lax.psum_scatter(
            projected(attended(jnp.zeros((), jnp.int32), 1), out_weight),
            "tensor",
            scatter_dimension=0,
            tiled=True,
        )
    theirs = attended(1 - tensor, shares)
    cuts = 4
    moved = [
        lax.ppermute(project(theirs, out_weight, cut, cuts), "tensor", [(0, 1), (1, 0)])
        for cut in range(cuts)
    ]
    part, _ = lax.optimization_barrier((tensor, theirs))
    mine = attended(part, shares)
    out = None
    for cut in range(cuts):
        out = project(mine, out_weight, cut, cuts, moved[cut], out)
    return out


def solution(mesh):
    placed = (
        P("context", "tensor"),
        P("context", "tensor"),
        P("context", "tensor"),
        P("tensor", None),
        P("tensor", None),
        P(),
        P("tensor", None),
    )
    return jax.shard_map(
        per_device,
        mesh=mesh,
        in_specs=placed,
        out_specs=P(("context", "tensor"), None),
        check_vma=False,
    )
```

```python
import functools

import jax
import jax.numpy as jnp
from jax import lax
from jax.experimental import pallas as pl
from jax.experimental.pallas import tpu as pltpu
from jax.sharding import PartitionSpec as P

QH = 32
KVH = 8
HD = 128
BLOCK = 64
GROUP = QH // KVH
SPAN = 8
WIDE = SPAN * BLOCK

floor_score = -1e30
exp2_scale = HD ** (-0.5) * 1.4426950408889634


def plan(vert_cols, slash_off, doc_ids, context, blocks):
    query_block = context * blocks + jnp.arange(blocks, dtype=jnp.int32)
    query_doc = lax.dynamic_slice_in_dim(doc_ids, context * blocks, blocks, 0)
    doc_start = jnp.sum((doc_ids[None, :] < query_doc[:, None]).astype(jnp.int32), axis=1)
    at = query_block[None, :, None]
    start = doc_start[None, :, None]
    slash_key = at - slash_off[:, None, :]
    slash_live = slash_key >= start
    column = jnp.broadcast_to(
        (vert_cols // BLOCK)[:, None, :], (vert_cols.shape[0], blocks, vert_cols.shape[1])
    )
    on_slash = jnp.any((at - column)[..., None] == slash_off[:, None, None, :], axis=-1)
    column_live = (column < at) & jnp.logical_not(on_slash & (column >= start))
    diagonal = jnp.broadcast_to(at, slash_key.shape[:2] + (1,))
    ids = jnp.concatenate([diagonal, slash_key, column], axis=-1)
    live = jnp.concatenate([diagonal >= 0, slash_live, column_live], axis=-1)
    seats = -(-ids.shape[-1] // SPAN) * SPAN
    order = jnp.arange(ids.shape[-1])
    seat = jnp.sum(
        (live[..., None, :] & (order[None, :] < order[:, None])).astype(jnp.int32), axis=-1
    )
    count = jnp.sum(live.astype(jnp.int32), axis=-1)
    chosen = live[..., None, :] & (seat[..., None, :] == jnp.arange(seats)[:, None])
    packed = jnp.sum(jnp.where(chosen, ids[..., None, :], 0), axis=-1)
    packed = jnp.where(jnp.arange(seats) < count[..., None], packed, at)
    return packed.reshape(-1), count.reshape(-1), seats


def attend_kernel(blocks, here, seats, part_ref, ids_ref, count_ref, q_ref, k_ref, v_ref, o_ref, s_ref):
    head = pl.program_id(0)
    lead = part_ref[0] * here

    def one(index, carry):
        pair = head * blocks + lead + index
        count = count_ref[pair]
        chunks = (count + SPAN - 1) // SPAN
        rows = pl.ds(pl.multiple_of(index * BLOCK, BLOCK), BLOCK)
        q = jnp.concatenate([q_ref[rows, g * HD:(g + 1) * HD] for g in range(GROUP)], axis=0)

        def gathered(ref, chunk):
            parts = []
            for j in range(SPAN):
                where = ids_ref[pair * seats + chunk * SPAN + j]
                parts.append(ref[pl.ds(pl.multiple_of(where * BLOCK, BLOCK), BLOCK), :])
            return jnp.concatenate(parts, axis=0)

        def whole(number):
            most = None
            for chunk in range(number):
                s = lax.dot_general(
                    q, gathered(k_ref, chunk), (((1,), (1,)), ((), ())),
                    preferred_element_type=jnp.float32,
                )
                lane = lax.broadcasted_iota(jnp.int32, s.shape, 1)
                if chunk == 0:
                    row = lax.broadcasted_iota(jnp.int32, s.shape, 0) % BLOCK
                    s = jnp.where((lane > row) & (lane < BLOCK), floor_score, s)
                if chunk == number - 1:
                    s = jnp.where(lane < (count - chunk * SPAN) * BLOCK, s, floor_score)
                s_ref[:, chunk * WIDE:(chunk + 1) * WIDE] = s
                for part in range(0, WIDE, HD):
                    piece = s[:, part:part + HD]
                    most = piece if most is None else jnp.maximum(most, piece)
            top = jnp.max(most, axis=1, keepdims=True)
            summed = None
            total = None
            for chunk in range(number):
                s = s_ref[:, chunk * WIDE:(chunk + 1) * WIDE]
                p = jnp.exp2((s - top) * exp2_scale)
                for part in range(0, WIDE, HD):
                    piece = p[:, part:part + HD]
                    total = piece if total is None else total + piece
                out = jnp.dot(
                    p.astype(jnp.bfloat16), gathered(v_ref, chunk),
                    preferred_element_type=jnp.float32,
                )
                summed = out if summed is None else summed + out
            out = (summed / jnp.sum(total, axis=1, keepdims=True)).astype(jnp.bfloat16)
            for g in range(GROUP):
                o_ref[rows, g * HD:(g + 1) * HD] = out[g * BLOCK:(g + 1) * BLOCK]

        for number in range(1, seats // SPAN + 1):
            pl.when(chunks == number)(functools.partial(whole, number))
        return carry

    lax.fori_loop(0, here, one, 0)


def attend(query, keys, values, part, parts, ids, count, seats):
    rows = query.shape[0] // parts
    heads = keys.shape[1] // HD
    tokens = keys.shape[0]
    grid_spec = pltpu.PrefetchScalarGridSpec(
        num_scalar_prefetch=3,
        grid=(heads,),
        in_specs=[
            pl.BlockSpec((rows, GROUP * HD), lambda h, part_ref, *_: (part_ref[0], h)),
            pl.BlockSpec((tokens, HD), lambda h, *_: (0, h)),
            pl.BlockSpec((tokens, HD), lambda h, *_: (0, h)),
        ],
        out_specs=pl.BlockSpec((rows, GROUP * HD), lambda h, *_: (0, h)),
        scratch_shapes=[pltpu.VMEM((GROUP * BLOCK, seats * BLOCK), jnp.float32)],
    )
    pairs = heads * rows * GROUP
    return pl.pallas_call(
        functools.partial(attend_kernel, query.shape[0] // BLOCK, rows // BLOCK, seats),
        grid_spec=grid_spec,
        out_shape=jax.ShapeDtypeStruct((rows, query.shape[1]), jnp.bfloat16),
        compiler_params=pltpu.CompilerParams(vmem_limit_bytes=48 * 1024 * 1024),
        cost_estimate=pl.CostEstimate(
            flops=4 * pairs * seats * BLOCK * HD,
            bytes_accessed=4 * tokens * heads * HD,
            transcendentals=pairs * seats * BLOCK,
        ),
        name="attend",
    )(part.reshape(1), ids, count, query, keys, values)


TILE = 512


def project_kernel(rows_ref, weight_ref, out_ref):
    part = jnp.dot(rows_ref[...], weight_ref[...], preferred_element_type=jnp.float32)
    out_ref[...] = part.astype(jnp.bfloat16)


def project(rows, weight, start, stop):
    height, depth = rows.shape
    columns = (stop - start) * TILE
    return pl.pallas_call(
        project_kernel,
        grid=(stop - start,),
        out_shape=jax.ShapeDtypeStruct((height, columns), rows.dtype),
        in_specs=[
            pl.BlockSpec((height, depth), lambda i: (0, 0)),
            pl.BlockSpec((depth, TILE), lambda i: (0, start + i)),
        ],
        out_specs=pl.BlockSpec((height, TILE), lambda i: (0, i)),
        compiler_params=pltpu.CompilerParams(vmem_limit_bytes=48 * 1024 * 1024),
        cost_estimate=pl.CostEstimate(
            flops=2 * height * depth * columns,
            bytes_accessed=2 * depth * columns,
            transcendentals=0,
        ),
        name="project",
    )(rows, weight)


LEVEL = 4


def gather_kernel(levels, k_ref, v_ref, gk_ref, gv_ref, send_sem, recv_sem, own_sem):
    rows = k_ref.shape[0]
    me = lax.axis_index("context")
    level = me // LEVEL
    side = (me // 2) % 2
    core = me % 2
    over = me + 2 - 4 * side
    twin = me + 1 - 2 * core
    last = level == levels - 1

    barrier = pltpu.get_barrier_semaphore()

    def greet(device):
        pl.semaphore_signal(
            barrier, inc=1, device_id={"context": device}, device_id_type=pl.DeviceIdType.MESH
        )

    greet(over)
    greet(twin)
    pl.when(level > 0)(lambda: greet(me - LEVEL))
    pl.when(level < levels - 1)(lambda: greet(me + LEVEL))
    pl.semaphore_wait(
        barrier, 2 + jnp.where(level > 0, 1, 0) + jnp.where(level < levels - 1, 1, 0)
    )

    inputs, gathered = (k_ref, v_ref), (gk_ref, gv_ref)

    def place(owner, part):
        return gathered[part].at[pl.ds(pl.multiple_of(owner * rows, rows), rows), :]

    def copy(owner, part, device, sem, own=False):
        return pltpu.make_async_remote_copy(
            src_ref=inputs[part] if own else place(owner, part),
            dst_ref=place(owner, part),
            send_sem=send_sem.at[sem],
            recv_sem=recv_sem.at[owner, part],
            device_id={"context": device},
            device_id_type=pl.DeviceIdType.MESH,
        )

    def sem_of(kind, step, part):
        return (kind * levels + step) * 2 + part

    sent = []

    def send(condition, *args, **kwargs):
        pl.when(condition)(lambda: copy(*args, **kwargs).start())
        sent.append((condition, args, kwargs))

    def arrive(condition, owner, part):
        pl.when(condition)(lambda: copy(owner, part, twin, 0).wait_recv())

    own_copies = [
        pltpu.make_async_copy(inputs[part], place(me, part), own_sem.at[part]) for part in range(2)
    ]
    for own_copy in own_copies:
        own_copy.start()

    climber = core
    for step in range(levels + 1):
        from_level = level - step
        if step < levels:
            held = from_level >= 0
            owner = from_level * LEVEL + side * 2 + core
            for part in range(2):
                if step:
                    arrive(held, owner, part)
                send(held & (level < levels - 1), owner, part, me + LEVEL, sem_of(0, step, part), own=step == 0)
                crosses = held & (side == 0) if step == 0 else held
                if part == 0 and step > 0:
                    crosses = crosses & jnp.logical_not((from_level == 0) & (side == 0))
                send(crosses, owner, part, over, sem_of(1, step, part), own=step == 0)
                send(held & (core == 0) if step == 0 else held, owner, part, twin, sem_of(2, step, part), own=step == 0)
        if step:
            back = step - 1
            before = level - back
            owner = before * LEVEL + (1 - side) * 2 + core
            for part in range(2):
                crossed = (before >= 0) & (side == 1) if back == 0 else before >= 0
                arrive(crossed, owner, part)
                if part == 0:
                    climbs = crossed & (before == 0) & (side == 1)
                    send(climbs & (level < levels - 1), owner, part, me + LEVEL, sem_of(4, back, part))
                send(crossed, owner, part, twin, sem_of(3, back, part))
    for before in range(levels):
        for other in range(2):
            for part in range(2):
                owner = before * LEVEL + other * 2 + 1 - core
                mine = (before == level) & ((other < side) | ((other == side) & (core == 1)))
                arrive((before < level) | mine, owner, part)
    for condition, args, kwargs in sent:
        pl.when(condition)(lambda args=args, kwargs=kwargs: copy(*args, **kwargs).wait_send())
    for own_copy in own_copies:
        own_copy.wait()


def gather(keys, values, count):
    levels = count // LEVEL
    shape = jax.ShapeDtypeStruct((count * keys.shape[0], keys.shape[1]), keys.dtype)
    return pl.pallas_call(
        functools.partial(gather_kernel, levels),
        out_shape=(shape, shape),
        in_specs=[pl.BlockSpec(memory_space=pl.ANY)] * 2,
        out_specs=(pl.BlockSpec(memory_space=pl.ANY),) * 2,
        scratch_shapes=[
            pltpu.SemaphoreType.DMA((5 * levels * 2,)),
            pltpu.SemaphoreType.DMA((count, 2)),
            pltpu.SemaphoreType.DMA((2,)),
        ],
        compiler_params=pltpu.CompilerParams(
            collective_id=0, has_side_effects=True, vmem_limit_bytes=60 * 1024 * 1024
        ),
        name="gather",
    )(keys, values)


def per_device(query, keys, values, vert_cols, slash_off, doc_ids, out_weight):
    blocks = keys.shape[0] // BLOCK
    context = lax.axis_index("context")
    tensor = lax.axis_index("tensor")
    shares = lax.axis_size("tensor")
    ids, count, seats = plan(vert_cols, slash_off, doc_ids, context, blocks)
    all_keys, all_values = gather(keys, values, lax.axis_size("context"))

    if shares != 2 or blocks % shares:
        first = jnp.zeros((), jnp.int32)
        rows = attend(query, all_keys, all_values, first, 1, ids, count, seats)
        return lax.psum_scatter(
            jnp.dot(rows, out_weight, preferred_element_type=jnp.float32).astype(jnp.bfloat16),
            "tensor",
            scatter_dimension=0,
            tiled=True,
        )
    theirs = attend(query, all_keys, all_values, 1 - tensor, shares, ids, count, seats)
    tiles = out_weight.shape[1] // TILE
    cut = 2
    moved = [
        lax.ppermute(project(theirs, out_weight, at, at + cut), "tensor", [(0, 1), (1, 0)])
        for at in range(0, tiles, cut)
    ]
    part, _ = lax.optimization_barrier((tensor, theirs))
    mine = attend(query, all_keys, all_values, part, shares, ids, count, seats)
    own = project(mine, out_weight, 0, tiles)
    return (
        own.astype(jnp.float32) + jnp.concatenate(moved, axis=1).astype(jnp.float32)
    ).astype(jnp.bfloat16)


def solution(mesh):
    placed = (
        P("context", "tensor"),
        P("context", "tensor"),
        P("context", "tensor"),
        P("tensor", None),
        P("tensor", None),
        P(),
        P("tensor", None),
    )
    return jax.shard_map(
        per_device,
        mesh=mesh,
        in_specs=placed,
        out_specs=P(("context", "tensor"), None),
        check_vma=False,
    )
```
